128 devices in a mesh: row: 8 (over z_hi, y), col: 16 (over x, z_lo, core).
Axes of the slice: x: 4, y: 4, z: 4 (z_hi: 2, z_lo: 2; z = z_hi * 2 + z_lo), core: 2. Of those that a mesh axis runs over, the one named last changes fastest.
Arguments:
- tiles: float32 [48, 32, 512, 512], P('row', 'col'), may hold values from -6 to 134, as said below
- pattern: int32 [2, 48], replicated, may hold values from 0 to 1, as said below
Outputs:
- factored: float32 [48, 32, 512, 512], P('row', 'col')
The draws below stay inside these ranges and needn't reach their ends.
Inputs may be any that keep to these rules, and one draw needn't show every extreme that they name: The window's diagonal tiles have 128 added to their diagonal entries; all other entries lie within -6 to 6. `pattern`: for each panel and each class of tile rows that share one device row, at most 5 of its 6 entries are 1, and exactly 5 for some class.
All inputs are finite; a program needn't handle non-finite values.
Results may differ from the reference program's by a relative error of at most 0.0014.
Values may be sent and summed in bfloat16 or wider, within the bound.
A program may use at most 192 MiB of HBM per device.

```python
import jax
import jax.numpy as jnp
from jax import lax

B = 512
TR_DEV = 6
TC_DEV = 2
PANELS = 2
FILL_MOST = 5
NT = 48
NC = 32
N_ROW = 8
N_COL = 16


def draw_tiles(key, part):
    key = jax.random.fold_in(key, 5)
    shape = (NT, NC, B, B)
    values = jnp.clip(jax.random.normal(key, shape, jnp.float32), -6.0, 6.0)
    stored_rows = jnp.arange(NT)
    global_row = stored_rows % TR_DEV * (NT // TR_DEV) + stored_rows // TR_DEV
    stored_cols = jnp.arange(NC)
    global_col = stored_cols % TC_DEV * (NC // TC_DEV) + stored_cols // TC_DEV
    on_diagonal = (global_row[:, None] == global_col[None, :]).astype(jnp.float32)
    return values + 128.0 * on_diagonal[:, :, None, None] * jnp.eye(B, dtype=jnp.float32)[None, None]


def draw_pattern(key, part):
    key = jax.random.fold_in(key, 11)
    classes = NT // TR_DEV
    key_counts, key_forced, key_ranks = jax.random.split(key, 3)
    lowest = max(FILL_MOST // 3, 1)
    counts = jax.random.randint(key_counts, (PANELS, classes), lowest, FILL_MOST + 1)
    forced = jax.random.randint(key_forced, (PANELS,), 0, classes)
    counts = jnp.where(jnp.arange(classes)[None, :] == forced[:, None], FILL_MOST, counts)
    rank_keys = jax.random.split(key_ranks, PANELS * classes)
    ranks = jax.vmap(lambda one_key: jax.random.permutation(one_key, TR_DEV))(rank_keys)
    ranks = ranks.reshape(PANELS, classes, TR_DEV)
    filled = (ranks < counts[:, :, None]).astype(jnp.int32)
    return jnp.transpose(filled, (0, 2, 1)).reshape(PANELS, NT)


def setup_inputs(seed: int = 0) -> dict:
    key_of = jax.random.split(jax.random.key(seed), 3)
    return {
        "tiles": draw_tiles(jax.random.fold_in(key_of[2], 71), 0),
        "pattern": draw_pattern(jax.random.fold_in(key_of[2], 71), 0),
    }


def solve_panel(factor_tile, column_block):
    return jax.vmap(lambda one_tile: jax.scipy.linalg.solve_triangular(factor_tile, one_tile.T, lower=True).T)(column_block)

def reference(tiles, pattern):
    tile_rows = jnp.arange(NT, dtype=jnp.int32)
    stored_at = tile_rows % N_ROW * TR_DEV + tile_rows // N_ROW
    columns = jnp.arange(NC, dtype=jnp.int32)
    col_stored_at = columns % N_COL * TC_DEV + columns // N_COL
    matrix = tiles[stored_at][:, col_stored_at]
    for panel_index in range(PANELS):
        used_all = pattern[panel_index] * (tile_rows > panel_index).astype(jnp.int32)
        factor_tile = jnp.linalg.cholesky(matrix[panel_index, panel_index])
        column_block = matrix[:, panel_index]
        solved = solve_panel(factor_tile, column_block)
        lowered = jnp.where((used_all > 0)[:, None, None], solved, jnp.zeros_like(solved))
        newcol = jnp.where((tile_rows > panel_index)[:, None, None], lowered, column_block)
        newcol = newcol.at[panel_index].set(factor_tile)
        matrix = matrix.at[:, panel_index].set(newcol)
        rounded = lowered.astype(jnp.bfloat16)
        col_tiles = rounded[:NC].astype(jnp.float32)
        col_used = used_all[:NC]

        def update(row_data):
            target, own_tile, flag, position = row_data
            product = jnp.einsum('ab,jcb->jac', own_tile.astype(jnp.float32), col_tiles, precision=lax.Precision.HIGHEST)
            selected = flag * col_used * (position >= columns).astype(jnp.int32) > 0
            return jnp.where(selected[:, None, None], target - product, target)
        matrix = lax.map(update, (matrix, rounded, used_all, tile_rows))
    stored_rows = jnp.arange(NT, dtype=jnp.int32)
    inverse = stored_rows % TR_DEV * N_ROW + stored_rows // TR_DEV
    stored_cols = jnp.arange(NC, dtype=jnp.int32)
    col_inverse = stored_cols % TC_DEV * N_COL + stored_cols // TC_DEV
    return matrix[inverse][:, col_inverse]
```

```python
import jax
import jax.numpy as jnp
from jax import lax
from jax.experimental import pallas as pl
from jax.experimental.pallas import tpu as pltpu
from jax.sharding import PartitionSpec as P

F32 = jnp.float32
BF16 = jnp.bfloat16
B = 512
SLOTS = 6
Q = 4
QR = B // Q
SHIFT = 128.0


def flip(bit):
    return 1 - bit


def lookup(table, index):
    total = jnp.int32(0)
    for value, entry in enumerate(table):
        if entry:
            total = total + jnp.where(index == value, entry, 0)
    return total


def member(values, index):
    hit = jnp.bool_(False)
    for value in values:
        hit = hit | (index == value)
    return hit


def row_tree(t):
    depth = {0: 0, 1 << t: 1}
    children = {0: [], 1: [], 2: []}
    children[t].append(0)
    for d in ((t + 1) % 3, (t + 2) % 3, t):
        for node in list(depth):
            other = node ^ (1 << d)
            if node != 0 and other not in depth:
                depth[other] = depth[node] + 1
                children[d].append(node)
    return [depth[v] for v in range(8)], [children[d] for d in range(3)]


def column_tree(sign):
    depth = [0] * 8
    children = [[], [], []]
    ahead, behind = (0, 1) if sign > 0 else (1, 0)

    def ring(z, start, base):
        children[ahead].append(z * 4 + start)
        first = (start + sign) % 4
        depth[z * 4 + first] = base + 1
        children[ahead].append(z * 4 + first)
        depth[z * 4 + (first + sign) % 4] = base + 2
        children[behind].append(z * 4 + start)
        depth[z * 4 + (start - sign) % 4] = base + 1

    ring(0, 0, 0)
    cross = sign % 4
    children[2].append(cross)
    depth[4 + cross] = 2
    ring(1, cross, 2)
    return depth, children


ROW_TREES = [row_tree(t) for t in range(3)]
COL_TREES = [column_tree(1), column_tree(-1)]
N_ROW_CHUNKS = 2 * Q
N_COL_CHUNKS = 2 * Q
COL_START = 6
DIAG_START = 6
STEPS = max(N_ROW_CHUNKS + 5, COL_START + N_COL_CHUNKS + 4)


def share_kernel(tiles, rows, cols, diag, stage, load_sem, row_recv, row_send, mate_recv, mate_send,
                 col_recv, col_send, diag_recv, diag_send):
    rank_row = lax.axis_index("row")
    rank_col = lax.axis_index("col")
    zh, y = rank_row // 4, rank_row % 4
    x, zl, core = rank_col // 4, (rank_col // 2) % 2, rank_col % 2
    root = rank_col < 2

    row_peers = (
        (x + 1 - 2 * (x % 2)) * 4 + zl * 2 + core,
        (3 - x) * 4 + zl * 2 + core,
        x * 4 + flip(zl) * 2 + core,
    )
    mate = x * 4 + zl * 2 + flip(core)
    col_peers = (
        zh * 4 + (y + 1) % 4,
        zh * 4 + (y + 3) % 4,
        flip(zh) * 4 + y,
    )

    for s in range(SLOTS):
        @pl.when(root)
        def _():
            pltpu.make_async_copy(tiles.at[s, 0], stage.at[s], load_sem.at[s]).start()

    barrier = pltpu.get_barrier_semaphore()
    for peer in row_peers + (mate,):
        pl.semaphore_signal(barrier, inc=1, device_id={"col": peer}, device_id_type=pl.DeviceIdType.MESH)
    for peer in col_peers:
        pl.semaphore_signal(barrier, inc=1, device_id={"row": peer}, device_id_type=pl.DeviceIdType.MESH)
    pl.semaphore_wait(barrier, 7)

    node = (x + x // 2) % 2 + 2 * (x // 2) + 4 * zl

    def home(rank):
        return (zh - rank // 4) % 2 * 4 + (y - rank % 4) % 4

    def remote(src, dst, send, recv, axis, peer):
        return pltpu.make_async_remote_copy(
            src_ref=src, dst_ref=dst, send_sem=send, recv_sem=recv,
            device_id={axis: peer}, device_id_type=pl.DeviceIdType.MESH)

    def row_copy(t, n, d):
        block = rows.at[core, t + 3 * (n // Q), n % Q]
        return remote(block, block, row_send.at[t, n, d], row_recv.at[t, n], "col", row_peers[d])

    def mate_copy(t, n, panel):
        block = rows.at[panel, t + 3 * (n // Q), n % Q]
        return remote(block, block, mate_send.at[t, n], mate_recv.at[t, n], "col", mate)

    def col_copy(p, n, d, source=None):
        block = cols.at[p, n // Q, n % Q]
        return remote(block if source is None else source, block, col_send.at[p, n, d], col_recv.at[p, n],
                      "row", col_peers[d])

    def diag_copy(w, n, d):
        block = diag.at[w, n]
        return remote(block, block, diag_send.at[w, n, d], diag_recv.at[w, n], "row", col_peers[d])

    col_node = home(rank_col % 8)
    diag_nodes = (home(0), home(1), home(1))
    diag_src = ((0, 0), (0, 1), (1, 1))

    def step(h):
        if h < N_ROW_CHUNKS:
            for t in range(3):
                slot, q = t + 3 * (h // Q), h % Q
                @pl.when(root)
                def _():
                    if q == 0:
                        pltpu.make_async_copy(tiles.at[slot, 0], stage.at[slot], load_sem.at[slot]).wait()
                    piece = stage[slot, q * QR:(q + 1) * QR, :]
                    if slot == 0:
                        on = ((rank_row == 0) & (rank_col == 0)) | ((rank_row == 1) & (rank_col == 1))
                        shift = jnp.where(on, SHIFT, 0.0)
                        here = lax.broadcasted_iota(jnp.int32, (QR, B), 0) + q * QR
                        there = lax.broadcasted_iota(jnp.int32, (QR, B), 1)
                        piece = piece - jnp.where(here == there, shift, 0.0)
                    rows[core, slot, q] = piece.astype(BF16)

        for t in range(3):
            depths, children = ROW_TREES[t]
            depth = lookup(depths, node)
            n = h - depth
            inside = (n >= 0) & (n < N_ROW_CHUNKS)

            @pl.when(inside & (depth > 0))
            def _():
                row_copy(t, n, 0).wait_recv()
            for d in range(3):
                if children[d]:
                    @pl.when(inside & member(children[d], node))
                    def _():
                        row_copy(t, n, d).start()

            @pl.when(inside)
            def _():
                mate_copy(t, n, core).start()
            before = n - 1

            @pl.when((before >= 0) & (before < N_ROW_CHUNKS))
            def _():
                mate_copy(t, before, flip(core)).wait_recv()

        for w in range(3):
            depths, children = COL_TREES[w % 2]
            depth = lookup(depths, diag_nodes[w])
            n = h - DIAG_START - depth
            inside = (n >= 0) & (n < Q)
            panel, _unused = diag_src[w]

            @pl.when(inside & (depth == 0))
            def _():
                diag[w, n] = rows[panel, 0, n]

            @pl.when(inside & (depth > 0))
            def _():
                diag_copy(w, n, 0).wait_recv()
            for d in range(3):
                @pl.when(inside & member(children[d], diag_nodes[w]))
                def _():
                    diag_copy(w, n, d).start()

        for p in range(2):
            depths, children = COL_TREES[p]
            depth = lookup(depths, col_node)
            n = h - COL_START - depth
            inside = (n >= 0) & (n < N_COL_CHUNKS)

            @pl.when(inside & (depth == 0))
            def _():
                cols[p, n // Q, n % Q] = rows[p, rank_col // 8 + 2 * (n // Q), n % Q]

            @pl.when(inside & (depth > 0))
            def _():
                col_copy(p, n, 0).wait_recv()
            for d in range(3):
                @pl.when(inside & member(children[d], col_node))
                def _():
                    col_copy(p, n, d).start()

    for h in range(STEPS):
        step(h)

    def row_end(n, carry):
        for t in range(3):
            for d in range(3):
                if ROW_TREES[t][1][d]:
                    @pl.when(member(ROW_TREES[t][1][d], node))
                    def _():
                        row_copy(t, n, d).wait_send()
            mate_copy(t, n, core).wait_send()
        for p in range(2):
            for d in range(3):
                @pl.when(member(COL_TREES[p][1][d], col_node))
                def _():
                    col_copy(p, n, d).wait_send()
        return carry

    lax.fori_loop(0, N_ROW_CHUNKS, row_end, 0)

    def diag_end(n, carry):
        for w in range(3):
            for d in range(3):
                @pl.when(member(COL_TREES[w % 2][1][d], diag_nodes[w]))
                def _():
                    diag_copy(w, n, d).wait_send()
        return carry

    lax.fori_loop(0, Q, diag_end, 0)


def share(tiles):
    vmem = pl.BlockSpec(memory_space=pltpu.VMEM)
    return pl.pallas_call(
        share_kernel,
        out_shape=[
            jax.ShapeDtypeStruct((2, SLOTS, Q, QR, B), BF16),
            jax.ShapeDtypeStruct((2, 2, Q, QR, B), BF16),
            jax.ShapeDtypeStruct((3, Q, QR, B), BF16),
        ],
        in_specs=[pl.BlockSpec(memory_space=pl.ANY)],
        out_specs=[vmem, vmem, vmem],
        scratch_shapes=[
            pltpu.VMEM((SLOTS, B, B), F32),
            pltpu.SemaphoreType.DMA((SLOTS,)),
            pltpu.SemaphoreType.DMA((3, N_ROW_CHUNKS)),
            pltpu.SemaphoreType.DMA((3, N_ROW_CHUNKS, 3)),
            pltpu.SemaphoreType.DMA((3, N_ROW_CHUNKS)),
            pltpu.SemaphoreType.DMA((3, N_ROW_CHUNKS)),
            pltpu.SemaphoreType.DMA((2, N_COL_CHUNKS)),
            pltpu.SemaphoreType.DMA((2, N_COL_CHUNKS, 3)),
            pltpu.SemaphoreType.DMA((3, Q)),
            pltpu.SemaphoreType.DMA((3, Q, 3)),
        ],
        compiler_params=pltpu.CompilerParams(
            collective_id=0, has_side_effects=True, vmem_limit_bytes=40 << 20),
        name="share",
    )(tiles)


def halves(a):
    high = a.astype(BF16)
    return high, (a - high.astype(F32)).astype(BF16)


def dot1(a, b, dims):
    return lax.dot_general(a, b, (dims, ((), ())), preferred_element_type=F32)


def dot3(a, b, dims):
    ah, al = halves(a)
    bh, bl = halves(b)
    return dot1(ah, bh, dims) + (dot1(ah, bl, dims) + dot1(al, bh, dims))


NN = ((1,), (0,))
TN = ((0,), (0,))
NT = ((1,), (1,))


def factor128(S):
    lane = lax.broadcasted_iota(jnp.int32, (8, 128), 1)
    sub = lax.broadcasted_iota(jnp.int32, (8, 128), 0)
    T = [jnp.where(lane == sub + 8 * h, 1.0, 0.0).astype(F32) for h in range(16)]
    S = list(S)
    upper, inverse = [], []

    def along(v, l):
        return jnp.broadcast_to(v[:, l:l + 1], (8, 128))

    def down(v, s):
        return jnp.broadcast_to(v[s:s + 1, :], (8, 128))

    for g in range(16):
        p = 8 * g
        multipliers = [[along(S[h], p + s) for s in range(8)] for h in range(g, 16)]
        c = list(multipliers[0])
        X, Y = S[g], T[g]
        RX = jnp.zeros((8, 128), F32)
        RY = RX
        for s in range(8):
            root = lax.rsqrt(down(c[s], s))
            inv = root * root
            xr, yr = down(X, s), down(Y, s)
            me = sub == s
            RX = jnp.where(me, xr * root, RX)
            RY = jnp.where(me, yr * root, RY)
            qx, qy = xr * inv, yr * inv
            X = jnp.where(me, qx, X - c[s] * qx)
            Y = jnp.where(me, qy, Y - c[s] * qy)
            for u in range(s + 1, 8):
                qc = down(c[u], s) * inv
                c[u] = jnp.where(me, qc, c[u] - c[s] * qc)
        upper.append(RX)
        inverse.append(RY)
        if g < 15:
            QX = [down(X, s) for s in range(8)]
            QY = [down(Y, s) for s in range(8)]
            for h in range(g + 1, 16):
                a, t = S[h], T[h]
                for s in range(8):
                    m = multipliers[h - g][s]
                    a = a - m * QX[s]
                    t = t - m * QY[s]
                S[h], T[h] = a, t
    return upper, inverse


def factor_tile(M, U, W128):
    for k in range(4):
        b = 128 * k
        upper, inverse = factor128([M[b + 8 * h:b + 8 * h + 8, b:b + 128] for h in range(16)])
        lane = lax.broadcasted_iota(jnp.int32, (8, 128), 1)
        sub = lax.broadcasted_iota(jnp.int32, (8, 128), 0)
        for h in range(16):
            U[b + 8 * h:b + 8 * h + 8, b:b + 128] = jnp.where(lane >= sub + 8 * h, upper[h], 0.0)
            W128[8 * h:8 * h + 8, :] = jnp.where(lane <= sub + 8 * h, inverse[h], 0.0)
        block = W128[...]
        M[b:b + 128, 512 + b:640 + b] = block
        R = dot3(block, M[b:b + 128, b + 128:b + 512], NN)
        M[b:b + 128, b + 128:b + 512] = R
        if k < 3:
            n = 384 - 128 * k
            U[b:b + 128, b + 128:512] = R[:, :n]
            wide = M[b:b + 128, b + 128:b + 640]
            for r in range(k + 1, 4):
                o = 128 * (r - k - 1)
                M[128 * r:128 * r + 128, b + 128:b + 640] -= dot3(R[:, o:o + 128], wide, TN)


def update_kernel(pattern, tiles, rows_in, cols_in, diag_in, out, rows, cols, diag, work, M, U0, U1, W128,
                  W0, W1, L1, sems, out_sem):
    rank_row = lax.axis_index("row")
    rank_col = lax.axis_index("col")

    loads = [
        pltpu.make_async_copy(diag_in, diag, sems.at[0]),
        pltpu.make_async_copy(rows_in, rows, sems.at[1]),
        pltpu.make_async_copy(cols_in, cols, sems.at[2]),
        pltpu.make_async_copy(tiles, work, sems.at[3]),
    ]
    for load in loads:
        load.start()

    here = lax.broadcasted_iota(jnp.int32, (B, B), 0)
    there = lax.broadcasted_iota(jnp.int32, (B, B), 1)
    eye = jnp.where(here == there, SHIFT, 0.0)

    def used(panel, i):
        return jnp.where(i > panel, pattern[panel, i], 0)

    def begin(a):
        M[:, 0:B] = 0.5 * (a + a.T) + eye
        M[:, B:2 * B] = jnp.zeros((B, B), F32)

    def finish(U, W):
        for k in range(1, 4):
            U[128 * k:128 * k + 128, 0:128 * k] = jnp.zeros((128, 128 * k), F32)
        high, low = halves(M[:, B:2 * B])
        W[0] = high
        W[1] = low

    def solve(a, W):
        return dot1(a, W[0], NT) + dot1(a, W[1], NT)

    loads[0].wait()
    begin(diag[0].astype(F32))
    factor_tile(M, U0, W128)
    finish(U0, W0)

    flag1 = used(0, 1).astype(F32)
    lead = (flag1 * solve(diag[1], W0)).astype(BF16)
    L1[...] = lead
    begin(diag[2].astype(F32) - dot1(lead, lead, NT))
    factor_tile(M, U1, W128)
    finish(U1, W1)

    loads[1].wait()
    loads[2].wait()
    loads[3].wait()

    def solve_both(ref, s, i, keep):
        first = used(0, i).astype(F32) * solve(ref[0, s], W0)
        first_b = first.astype(BF16)
        second_a = ref[1, s].astype(F32) - dot1(first_b, L1[...], NT)
        second = used(1, i).astype(F32) * solve(second_a.astype(BF16), W1)
        ref[0, s] = first_b
        ref[1, s] = second.astype(BF16)
        if keep:
            @pl.when((rank_col == 0) & (i > 0))
            def _():
                work[s, 0] = first

            @pl.when((rank_col == 1) & (i > 1))
            def _():
                work[s, 0] = second

    for k in range(2):
        solve_both(cols, k, rank_col + 16 * k, False)

    def one_row(s, carry):
        i = rank_row + 8 * s
        solve_both(rows, s, i, True)
        for k in range(2):
            j = rank_col + 16 * k
            for p in range(2):
                on = (j > 1) & (i >= j) & (used(p, i) > 0) & (used(p, j) > 0)

                @pl.when(on)
                def _():
                    work[s, k] -= dot1(rows[p, s], cols[p, k], NT)
        @pl.when((rank_col == 0) & (i == 0))
        def _():
            work[s, 0] = U0[...].T

        @pl.when((rank_col == 1) & (i == 1))
        def _():
            work[s, 0] = U1[...].T
        pltpu.make_async_copy(work.at[s], out.at[s], out_sem.at[s]).start()
        return carry

    lax.fori_loop(0, SLOTS, one_row, 0)
    for s in range(SLOTS):
        pltpu.make_async_copy(work.at[s], out.at[s], out_sem.at[s]).wait()


def update(pattern, tiles, rows, cols, diag):
    hbm = pl.BlockSpec(memory_space=pl.ANY)
    return pl.pallas_call(
        update_kernel,
        out_shape=jax.ShapeDtypeStruct(tiles.shape, F32),
        in_specs=[pl.BlockSpec(memory_space=pltpu.SMEM), hbm, hbm, hbm, hbm],
        out_specs=hbm,
        scratch_shapes=[
            pltpu.VMEM((2, SLOTS, B, B), BF16),
            pltpu.VMEM((2, 2, B, B), BF16),
            pltpu.VMEM((3, B, B), BF16),
            pltpu.VMEM((SLOTS, 2, B, B), F32),
            pltpu.VMEM((B, 2 * B), F32),
            pltpu.VMEM((B, B), F32),
            pltpu.VMEM((B, B), F32),
            pltpu.VMEM((128, 128), F32),
            pltpu.VMEM((2, B, B), BF16),
            pltpu.VMEM((2, B, B), BF16),
            pltpu.VMEM((B, B), BF16),
            pltpu.SemaphoreType.DMA((4,)),
            pltpu.SemaphoreType.DMA((SLOTS,)),
        ],
        compiler_params=pltpu.CompilerParams(vmem_limit_bytes=56 << 20),
        name="update",
    )(pattern, tiles, rows, cols, diag)


def per_device(tiles, pattern):
    rows, cols, diag = share(tiles)
    return update(
        pattern, tiles,
        rows.reshape(2, SLOTS, B, B), cols.reshape(2, 2, B, B), diag.reshape(3, B, B))


def solution(mesh):
    placed = P("row", "col", None, None)
    return jax.shard_map(
        per_device,
        mesh=mesh,
        in_specs=(placed, P()),
        out_specs=placed,
        check_vma=False,
    )
```

```python
import jax
import jax.numpy as jnp
from jax import lax
from jax.experimental import pallas as pl
from jax.experimental.pallas import tpu as pltpu
from jax.sharding import PartitionSpec as P

F32 = jnp.float32
BF16 = jnp.bfloat16
B = 512
SLOTS = 6
Q = 4
QR = B // Q
SHIFT = 128.0


def flip(bit):
    return 1 - bit


def lookup(table, index):
    total = jnp.int32(0)
    for value, entry in enumerate(table):
        if entry:
            total = total + jnp.where(index == value, entry, 0)
    return total


def member(values, index):
    hit = jnp.bool_(False)
    for value in values:
        hit = hit | (index == value)
    return hit


def row_tree(t):
    depth = {0: 0, 1 << t: 1}
    children = {0: [], 1: [], 2: []}
    children[t].append(0)
    for d in ((t + 1) % 3, (t + 2) % 3, t):
        for node in list(depth):
            other = node ^ (1 << d)
            if node != 0 and other not in depth:
                depth[other] = depth[node] + 1
                children[d].append(node)
    return [depth[v] for v in range(8)], [children[d] for d in range(3)]


def column_tree(sign, cross):
    depth = [0] * 8
    children = [[], [], []]
    ahead, behind = (0, 1) if sign > 0 else (1, 0)

    def ring(z, start, base):
        children[ahead].append(z * 4 + start)
        first = (start + sign) % 4
        depth[z * 4 + first] = base + 1
        children[ahead].append(z * 4 + first)
        depth[z * 4 + (first + sign) % 4] = base + 2
        children[behind].append(z * 4 + start)
        depth[z * 4 + (start - sign) % 4] = base + 1

    ring(0, 0, 0)
    children[2].append(cross)
    depth[4 + cross] = depth[cross] + 1
    ring(1, cross, depth[cross] + 1)
    return depth, children


ROW_TREES = [row_tree(t) for t in range(3)]
COL_TREES = [[column_tree(sign, 0), column_tree(sign, sign % 4)] for sign in (-1, 1)]
N_ROW = 2 * Q
N_COL = 2 * Q
COL_START = 5
STEPS = max(N_ROW + 5, COL_START + N_COL + 4)
UPPER = [(i, j) for i in range(4) for j in range(i, 4)]
ROW_FROM = 8
ROW_EVERY = 2
HOOK_GROUPS = (3, 7, 11, 15)


def front_kernel(pattern, tiles, rows_out, cols_out, F_out, W_out, L_out,
                 rows, cols, stage, a00, a10, a11, M, U0, U1, W128, W, L1,
                 load_sem, out_sem, row_recv, row_send, mate_recv, mate_send, col_recv, col_send,
                 d0_recv, d0_send, d1_recv, d1_send, d2_recv, d2_send):
    rank_row = lax.axis_index("row")
    rank_col = lax.axis_index("col")
    zh, y = rank_row // 4, rank_row % 4
    x, zl, core = rank_col // 4, (rank_col // 2) % 2, rank_col % 2
    z = zh * 2 + zl
    root = rank_col < 2

    def at(x1, y1, z1, core1):
        return ((z1 // 2) * 4 + y1, x1 * 4 + (z1 % 2) * 2 + core1)

    x_next, x_last = at((x + 1) % 4, y, z, core), at((x + 3) % 4, y, z, core)
    y_next, y_last = at(x, (y + 1) % 4, z, core), at(x, (y + 3) % 4, z, core)
    z_next, z_last = at(x, y, (z + 1) % 4, core), at(x, y, (z + 3) % 4, core)
    mate = at(x, y, z, flip(core))
    far = at(x, y, (z + 2) % 4, core)
    row_peers = (
        at(x + 1 - 2 * (x % 2), y, z, core),
        at(3 - x, y, z, core),
        at(x, y, z + 1 - 2 * zl, core),
    )
    col_peers = (y_next, y_last, far)

    for s in range(SLOTS):
        @pl.when(root)
        def _():
            pltpu.make_async_copy(tiles.at[s, 0], stage.at[s], load_sem.at[s]).start()

    barrier = pltpu.get_barrier_semaphore()
    everyone = (x_next, x_last, y_next, y_last, z_next, z_last, mate, far)
    for peer in everyone:
        pl.semaphore_signal(barrier, inc=1, device_id=peer, device_id_type=pl.DeviceIdType.MESH)
    pl.semaphore_wait(barrier, len(everyone))

    node = (x + x // 2) % 2 + 2 * (x // 2) + 4 * zl

    def home(rank):
        return (zh - rank // 4) % 2 * 4 + (y - rank % 4) % 4

    def remote(src, dst, send, recv, peer):
        return pltpu.make_async_remote_copy(
            src_ref=src, dst_ref=dst, send_sem=send, recv_sem=recv,
            device_id=peer, device_id_type=pl.DeviceIdType.MESH)

    def paced(cond, n, total, copy):
        @pl.when(cond & (n >= 2) & (n < total + 2))
        def _():
            copy(n - 2).wait_send()

        @pl.when(cond & (n >= 0) & (n < total))
        def _():
            copy(n).start()

    class Near:
        def __init__(self, buf, total, y0, plane, recv, send):
            self.buf, self.total, self.recv, self.send = buf, total, recv, send
            dy = (y - y0) % 4

            def hops(d):
                return jnp.where(d == 0, 0, jnp.where(d == 2, 2, 1))

            self.mine = core == plane
            self.depth = hops(z) + hops(x) + hops(dy)
            on_z = (x == 0) & (dy == 0) & self.mine
            on_x = (dy == 0) & self.mine
            self.ways = [
                (z_next, on_z & (z < 2)), (z_last, on_z & (z == 0)),
                (x_next, on_x & (x < 2)), (x_last, on_x & (x == 0)),
                (y_next, self.mine & (dy < 2)), (y_last, self.mine & (dy == 0)),
                (mate, self.mine),
            ]
            self.last = total + 6 + 1 + 2

        def copy(self, n, way):
            return remote(self.buf.at[n], self.buf.at[n], self.send.at[n, way], self.recv.at[n], self.ways[way][0])

        def step(self, h):
            n = h - self.depth - jnp.where(self.mine, 0, 1)
            inside = (n >= 0) & (n < self.total)

            @pl.when(inside & ((self.depth > 0) | jnp.logical_not(self.mine)))
            def _():
                self.copy(n, 0).wait_recv()
            for way in range(7):
                paced(self.ways[way][1], n, self.total, lambda m, way=way: self.copy(m, way))

    near0 = Near(a00, 5, 0, 0, d0_recv, d0_send)
    near1 = Near(a10, 4, 1, 0, d1_recv, d1_send)
    near2 = Near(a11, 5, 1, 1, d2_recv, d2_send)

    here = lax.broadcasted_iota(jnp.int32, (B, B), 0)
    there = lax.broadcasted_iota(jnp.int32, (B, B), 1)

    def put_upper(buf):
        a = stage[0]
        a = (0.5 * (a + a.T) - jnp.where(here == there, SHIFT, 0.0)).astype(BF16)
        for e, (i, j) in enumerate(UPPER):
            buf[e // 2, e % 2] = a[128 * i:128 * i + 128, 128 * j:128 * j + 128]

    @pl.when(root)
    def _():
        pltpu.make_async_copy(tiles.at[0, 0], stage.at[0], load_sem.at[0]).wait()

    @pl.when((rank_row == 0) & (rank_col == 0))
    def _():
        put_upper(a00)

    @pl.when((rank_row == 1) & (rank_col == 1))
    def _():
        put_upper(a11)

    @pl.when((rank_row == 1) & (rank_col == 0))
    def _():
        for q in range(Q):
            a10[q] = stage[0, q * QR:(q + 1) * QR, :].astype(BF16)

    def near0_step(h, carry):
        near0.step(h)
        return carry

    lax.fori_loop(0, near0.last, near0_step, 0)

    def row_copy(t, n, d):
        block = rows.at[core, t + 3 * (n // Q), n % Q]
        return remote(block, block, row_send.at[t, n, d], row_recv.at[t, n], row_peers[d])

    def mate_copy(t, n, panel):
        block = rows.at[panel, t + 3 * (n // Q), n % Q]
        return remote(block, block, mate_send.at[t, n], mate_recv.at[t, n], mate)

    def col_copy(p, n, d):
        block = cols.at[p, n // Q, n % Q]
        return remote(block, block, col_send.at[p, n, d], col_recv.at[p, n], col_peers[d])

    col_node = home(rank_col % 8)
    row_depth = [lookup(ROW_TREES[t][0], node) for t in range(3)]
    row_child = [[member(ROW_TREES[t][1][d], node) for d in range(3)] for t in range(3)]
    even = core == 0
    col_depth = [jnp.where(even, lookup(COL_TREES[0][p][0], col_node), lookup(COL_TREES[1][p][0], col_node))
                 for p in range(2)]
    col_child = [[(even & member(COL_TREES[0][p][1][d], col_node))
                  | (jnp.logical_not(even) & member(COL_TREES[1][p][1][d], col_node)) for d in range(3)]
                 for p in range(2)]

    def bulk(h):
        if h < N_ROW:
            q = h % Q
            for t in range(3):
                slot = t + 3 * (h // Q)

                @pl.when(root)
                def _():
                    if q == 0 and slot > 0:
                        pltpu.make_async_copy(tiles.at[slot, 0], stage.at[slot], load_sem.at[slot]).wait()
                    rows[core, slot, q] = stage[slot, q * QR:(q + 1) * QR, :].astype(BF16)

        for t in range(3):
            if h < N_ROW + 6:
                n = h - row_depth[t]

                @pl.when((n >= 0) & (n < N_ROW) & (row_depth[t] > 0))
                def _():
                    row_copy(t, n, 0).wait_recv()
                for d in range(3):
                    paced(row_child[t][d], n, N_ROW, lambda m, d=d: row_copy(t, m, d))

                @pl.when((n >= 0) & (n < N_ROW))
                def _():
                    mate_copy(t, n, core).start()
                before = n - 1

                @pl.when((before >= 0) & (before < N_ROW))
                def _():
                    mate_copy(t, before, flip(core)).wait_recv()

        if h >= COL_START:
            for p in range(2):
                n = h - COL_START - col_depth[p]
                inside = (n >= 0) & (n < N_COL)

                @pl.when(inside & (col_depth[p] == 0))
                def _():
                    cols[p, n // Q, n % Q] = rows[p, rank_col // 8 + 2 * (n // Q), n % Q]

                @pl.when(inside & (col_depth[p] > 0))
                def _():
                    col_copy(p, n, 0).wait_recv()
                for d in range(3):
                    paced(col_child[p][d], n, N_COL, lambda m, d=d: col_copy(p, m, d))

    count = [0, 0]

    def hook():
        c = count[0]
        count[0] += 1
        if c < max(near1.last, near2.last):
            near1.step(c)
            near2.step(c)
        if c >= ROW_FROM and (c - ROW_FROM) % ROW_EVERY == 0 and count[1] < STEPS:
            bulk(count[1])
            count[1] += 1

    def used(panel, i):
        return jnp.where(i > panel, pattern[panel, i], 0)

    def begin(get):
        M[:, B:2 * B] = jnp.zeros((B, B), F32)
        for i, j in UPPER:
            block = get(i, j)
            if i == j:
                block = block + jnp.where(here[:128, :128] == there[:128, :128], SHIFT, 0.0)
            M[128 * i:128 * i + 128, 128 * j:128 * j + 128] = block

    def finish(U, w):
        for k in range(1, 4):
            U[128 * k:128 * k + 128, 0:128 * k] = jnp.zeros((128, 128 * k), F32)
        W[w] = M[:, B:2 * B].astype(BF16)

    begin(lambda i, j: a00[UPPER.index((i, j)) // 2, UPPER.index((i, j)) % 2].astype(F32))
    factor_tile(M, U0, W128, hook)
    finish(U0, 0)
    while count[0] < max(near1.last, near2.last):
        hook()
    lead = (used(0, 1).astype(F32) * dot1(a10[...].reshape(B, B), W[0], NT)).astype(BF16)
    L1[...] = lead

    def second(i, j):
        e = UPPER.index((i, j))
        return a11[e // 2, e % 2].astype(F32) - dot1(
            L1[128 * i:128 * i + 128, :], L1[128 * j:128 * j + 128, :], NT)

    begin(second)
    factor_tile(M, U1, W128, hook)
    finish(U1, 1)

    ends = [
        pltpu.make_async_copy(U0, F_out.at[0], out_sem.at[0]),
        pltpu.make_async_copy(U1, F_out.at[1], out_sem.at[1]),
        pltpu.make_async_copy(W, W_out, out_sem.at[2]),
        pltpu.make_async_copy(L1, L_out, out_sem.at[3]),
    ]
    for end in ends:
        end.start()
    while count[1] < STEPS:
        bulk(count[1])
        count[1] += 1
    more = [
        pltpu.make_async_copy(rows, rows_out, out_sem.at[4]),
        pltpu.make_async_copy(cols, cols_out, out_sem.at[5]),
    ]
    for end in more:
        end.start()

    def mates(n, carry):
        for t in range(3):
            mate_copy(t, n, core).wait_send()
        return carry

    lax.fori_loop(0, N_ROW, mates, 0)
    for p in range(2):
        for d in range(3):
            for n in (N_COL - 2, N_COL - 1):
                late = n + 2 + COL_START + col_depth[p] >= STEPS

                @pl.when(col_child[p][d] & late)
                def _():
                    col_copy(p, n, d).wait_send()
    for end in ends + more:
        end.wait()


def front(pattern, tiles):
    hbm = pl.BlockSpec(memory_space=pl.ANY)
    dma = pltpu.SemaphoreType.DMA
    return pl.pallas_call(
        front_kernel,
        out_shape=[
            jax.ShapeDtypeStruct((2, SLOTS, Q, QR, B), BF16),
            jax.ShapeDtypeStruct((2, 2, Q, QR, B), BF16),
            jax.ShapeDtypeStruct((2, B, B), F32),
            jax.ShapeDtypeStruct((2, B, B), BF16),
            jax.ShapeDtypeStruct((B, B), BF16),
        ],
        in_specs=[pl.BlockSpec(memory_space=pltpu.SMEM), hbm],
        out_specs=[hbm] * 5,
        scratch_shapes=[
            pltpu.VMEM((2, SLOTS, Q, QR, B), BF16),
            pltpu.VMEM((2, 2, Q, QR, B), BF16),
            pltpu.VMEM((SLOTS, B, B), F32),
            pltpu.VMEM((5, 2, 128, 128), BF16),
            pltpu.VMEM((Q, QR, B), BF16),
            pltpu.VMEM((5, 2, 128, 128), BF16),
            pltpu.VMEM((B, 2 * B), F32),
            pltpu.VMEM((B, B), F32),
            pltpu.VMEM((B, B), F32),
            pltpu.VMEM((128, 128), F32),
            pltpu.VMEM((2, B, B), BF16),
            pltpu.VMEM((B, B), BF16),
            dma((SLOTS,)),
            dma((6,)),
            dma((3, N_ROW)),
            dma((3, N_ROW, 3)),
            dma((3, N_ROW)),
            dma((3, N_ROW)),
            dma((2, N_COL)),
            dma((2, N_COL, 3)),
            dma((5,)),
            dma((5, 7)),
            dma((4,)),
            dma((4, 7)),
            dma((5,)),
            dma((5, 7)),
        ],
        compiler_params=pltpu.CompilerParams(
            collective_id=0, has_side_effects=True, vmem_limit_bytes=48 << 20),
        name="front",
    )(pattern, tiles)


def halves(a):
    high = a.astype(BF16)
    return high, (a - high.astype(F32)).astype(BF16)


def dot1(a, b, dims):
    return lax.dot_general(a, b, (dims, ((), ())), preferred_element_type=F32)


def dot3(a, b, dims):
    ah, al = halves(a)
    bh, bl = halves(b)
    return dot1(ah, bh, dims) + (dot1(ah, bl, dims) + dot1(al, bh, dims))


NN = ((1,), (0,))
TN = ((0,), (0,))
NT = ((1,), (1,))


def factor128(S, hook):
    lane = lax.broadcasted_iota(jnp.int32, (8, 128), 1)
    sub = lax.broadcasted_iota(jnp.int32, (8, 128), 0)
    T = [jnp.where(lane == sub + 8 * h, 1.0, 0.0).astype(F32) for h in range(16)]
    S = list(S)
    upper, inverse = [], []

    def along(v, l):
        return jnp.broadcast_to(v[:, l:l + 1], (8, 128))

    def down(v, s):
        return jnp.broadcast_to(v[s:s + 1, :], (8, 128))

    for g in range(16):
        p = 8 * g
        multipliers = [[along(S[h], p + s) for s in range(8)] for h in range(g, 16)]
        c = list(multipliers[0])
        X, Y = S[g], T[g]
        RX = jnp.zeros((8, 128), F32)
        RY = RX
        for s in range(8):
            root = lax.rsqrt(down(c[s], s))
            inv = root * root
            xr, yr = down(X, s), down(Y, s)
            me = sub == s
            RX = jnp.where(me, xr * root, RX)
            RY = jnp.where(me, yr * root, RY)
            qx, qy = xr * inv, yr * inv
            X = jnp.where(me, qx, X - c[s] * qx)
            Y = jnp.where(me, qy, Y - c[s] * qy)
            for u in range(s + 1, 8):
                qc = down(c[u], s) * inv
                c[u] = jnp.where(me, qc, c[u] - c[s] * qc)
        upper.append(RX)
        inverse.append(RY)
        if g in HOOK_GROUPS:
            hook()
        if g < 15:
            QX = [down(X, s) for s in range(8)]
            QY = [down(Y, s) for s in range(8)]
            for h in range(g + 1, 16):
                a, t = S[h], T[h]
                for s in range(8):
                    m = multipliers[h - g][s]
                    a = a - m * QX[s]
                    t = t - m * QY[s]
                S[h], T[h] = a, t
    return upper, inverse


def factor_tile(M, U, W128, hook):
    for k in range(4):
        b = 128 * k
        upper, inverse = factor128([M[b + 8 * h:b + 8 * h + 8, b:b + 128] for h in range(16)], hook)
        lane = lax.broadcasted_iota(jnp.int32, (8, 128), 1)
        sub = lax.broadcasted_iota(jnp.int32, (8, 128), 0)
        for h in range(16):
            U[b + 8 * h:b + 8 * h + 8, b:b + 128] = jnp.where(lane >= sub + 8 * h, upper[h], 0.0)
            W128[8 * h:8 * h + 8, :] = jnp.where(lane <= sub + 8 * h, inverse[h], 0.0)
        block = W128[...]
        M[b:b + 128, 512 + b:640 + b] = block
        R = dot3(block, M[b:b + 128, b + 128:b + 512], NN)
        M[b:b + 128, b + 128:b + 512] = R
        if k < 3:
            n = 384 - 128 * k
            U[b:b + 128, b + 128:512] = R[:, :n]
            wide = M[b:b + 128, b + 128:b + 640]
            for r in range(k + 1, 4):
                o = 128 * (r - k - 1)
                M[128 * r:128 * r + 128, b + 128:b + 640] -= dot3(R[:, o:o + 128], wide, TN)


def update_kernel(pattern, tiles, rows_in, cols_in, F_in, W_in, L_in, out, rows, cols, F, W, L1, work, sems, out_sem):
    rank_row = lax.axis_index("row")
    rank_col = lax.axis_index("col")

    loads = [
        pltpu.make_async_copy(W_in, W, sems.at[0]),
        pltpu.make_async_copy(rows_in, rows, sems.at[1]),
        pltpu.make_async_copy(cols_in, cols, sems.at[2]),
        pltpu.make_async_copy(L_in, L1, sems.at[3]),
        pltpu.make_async_copy(F_in, F, sems.at[4]),
        pltpu.make_async_copy(tiles, work, sems.at[5]),
    ]
    for load in loads:
        load.start()

    def used(panel, i):
        return jnp.where(i > panel, pattern[panel, i], 0)

    def solve(a, w):
        return dot1(a, W[w], NT)

    for load in loads:
        load.wait()

    def solve_both(ref, s, i, keep):
        first = used(0, i).astype(F32) * solve(ref[0, s], 0)
        first_b = first.astype(BF16)
        second_a = ref[1, s].astype(F32) - dot1(first_b, L1[...], NT)
        second = used(1, i).astype(F32) * solve(second_a.astype(BF16), 1)
        ref[0, s] = first_b
        ref[1, s] = second.astype(BF16)
        if keep:
            @pl.when((rank_col == 0) & (i > 0))
            def _():
                work[s, 0] = first

            @pl.when((rank_col == 1) & (i > 1))
            def _():
                work[s, 0] = second

    for k in range(2):
        solve_both(cols, k, rank_col + 16 * k, False)

    def one_row(s, carry):
        i = rank_row + 8 * s
        solve_both(rows, s, i, True)
        for k in range(2):
            j = rank_col + 16 * k
            for p in range(2):
                on = (j > 1) & (i >= j) & (used(p, i) > 0) & (used(p, j) > 0)

                @pl.when(on)
                def _():
                    work[s, k] -= dot1(rows[p, s], cols[p, k], NT)
        @pl.when((rank_col == 0) & (i == 0))
        def _():
            work[s, 0] = F[0].T

        @pl.when((rank_col == 1) & (i == 1))
        def _():
            work[s, 0] = F[1].T
        pltpu.make_async_copy(work.at[s], out.at[s], out_sem.at[s]).start()
        return carry

    lax.fori_loop(0, SLOTS, one_row, 0)
    for s in range(SLOTS):
        pltpu.make_async_copy(work.at[s], out.at[s], out_sem.at[s]).wait()


def update(pattern, tiles, *found):
    hbm = pl.BlockSpec(memory_space=pl.ANY)
    return pl.pallas_call(
        update_kernel,
        out_shape=jax.ShapeDtypeStruct(tiles.shape, F32),
        in_specs=[pl.BlockSpec(memory_space=pltpu.SMEM)] + [hbm] * 6,
        out_specs=hbm,
        scratch_shapes=[
            pltpu.VMEM((2, SLOTS, B, B), BF16),
            pltpu.VMEM((2, 2, B, B), BF16),
            pltpu.VMEM((2, B, B), F32),
            pltpu.VMEM((2, B, B), BF16),
            pltpu.VMEM((B, B), BF16),
            pltpu.VMEM((SLOTS, 2, B, B), F32),
            pltpu.SemaphoreType.DMA((6,)),
            pltpu.SemaphoreType.DMA((SLOTS,)),
        ],
        compiler_params=pltpu.CompilerParams(vmem_limit_bytes=48 << 20),
        name="update",
    )(pattern, tiles, *found)


def per_device(tiles, pattern):
    rows, cols, factors, inverses, lead = front(pattern, tiles)
    return update(
        pattern, tiles, rows.reshape(2, SLOTS, B, B), cols.reshape(2, 2, B, B), factors, inverses, lead)


def solution(mesh):
    placed = P("row", "col", None, None)
    return jax.shard_map(
        per_device,
        mesh=mesh,
        in_specs=(placed, P()),
        out_specs=placed,
        check_vma=False,
    )
```

```python
import jax
import jax.numpy as jnp
from jax import lax
from jax.experimental import pallas as pl
from jax.experimental.pallas import tpu as pltpu
from jax.sharding import PartitionSpec as P

F32 = jnp.float32
BF16 = jnp.bfloat16
B = 512
SLOTS = 6
Q = 4
QR = B // Q
SHIFT = 128.0


def flip(bit):
    return 1 - bit


def lookup(table, index):
    total = jnp.int32(0)
    for value, entry in enumerate(table):
        if entry:
            total = total + jnp.where(index == value, entry, 0)
    return total


def member(values, index):
    hit = jnp.bool_(False)
    for value in values:
        hit = hit | (index == value)
    return hit


def row_tree(t):
    depth = {0: 0, 1 << t: 1}
    children = {0: [], 1: [], 2: []}
    children[t].append(0)
    for d in ((t + 1) % 3, (t + 2) % 3, t):
        for node in list(depth):
            other = node ^ (1 << d)
            if node != 0 and other not in depth:
                depth[other] = depth[node] + 1
                children[d].append(node)
    return [depth[v] for v in range(8)], [children[d] for d in range(3)]


def column_tree(sign, cross):
    depth = [0] * 8
    children = [[], [], []]
    ahead, behind = (0, 1) if sign > 0 else (1, 0)

    def ring(z, start, base):
        children[ahead].append(z * 4 + start)
        first = (start + sign) % 4
        depth[z * 4 + first] = base + 1
        children[ahead].append(z * 4 + first)
        depth[z * 4 + (first + sign) % 4] = base + 2
        children[behind].append(z * 4 + start)
        depth[z * 4 + (start - sign) % 4] = base + 1

    ring(0, 0, 0)
    children[2].append(cross)
    depth[4 + cross] = depth[cross] + 1
    ring(1, cross, depth[cross] + 1)
    return depth, children


ROW_TREES = [row_tree(t) for t in range(3)]
COL_TREES = [[column_tree(sign, 0), column_tree(sign, sign % 4)] for sign in (-1, 1)]
N_ROW = 2 * Q
N_COL = 2 * Q
LAG = 2
COL_START = 3 * LAG + 1
SECOND = (4, 3, 5)
ROW_STEPS = N_ROW + 4 * LAG + 1
STEPS = COL_START + N_COL + 4 * LAG
UPPER = [(i, j) for i in range(4) for j in range(i, 4)]
HOOK_GROUPS = (1, 3, 5, 7, 9, 11, 13, 15)
HOOKS = 4 * len(HOOK_GROUPS)
FIRST_UNITS = 11
BULK_HOOKS = 4


def front_kernel(pattern, tiles, rows_out, cols_out, F_out, W_out, L_out,
                 rows, cols, solved, stage, a00, a10, a11, M, U0, U1, W128, W, L1,
                 load_sem, out_sem, row_out_sem, row_recv, row_send, mate_recv, mate_send, col_recv, col_send,
                 d0_recv, d0_send, d1_recv, d1_send, d2_recv, d2_send):
    rank_row = lax.axis_index("row")
    rank_col = lax.axis_index("col")
    zh, y = rank_row // 4, rank_row % 4
    x, zl, core = rank_col // 4, (rank_col // 2) % 2, rank_col % 2
    z = zh * 2 + zl
    root = rank_col < 2

    def at(x1, y1, z1, core1):
        return ((z1 // 2) * 4 + y1, x1 * 4 + (z1 % 2) * 2 + core1)

    x_next, x_last = at((x + 1) % 4, y, z, core), at((x + 3) % 4, y, z, core)
    y_next, y_last = at(x, (y + 1) % 4, z, core), at(x, (y + 3) % 4, z, core)
    z_next, z_last = at(x, y, (z + 1) % 4, core), at(x, y, (z + 3) % 4, core)
    mate = at(x, y, z, flip(core))
    far = at(x, y, (z + 2) % 4, core)
    x_far, y_far = at((x + 2) % 4, y, z, core), at(x, (y + 2) % 4, z, core)
    row_peers = (
        at(x + 1 - 2 * (x % 2), y, z, core),
        at(3 - x, y, z, core),
        at(x, y, z + 1 - 2 * zl, core),
    )
    col_peers = (y_next, y_last, far)

    def load(s):
        return pltpu.make_async_copy(tiles.at[s, 0], stage.at[s], load_sem.at[s])

    @pl.when(root)
    def _():
        load(0).start()

    barrier = pltpu.get_barrier_semaphore()
    everyone = (x_next, x_last, x_far, y_next, y_last, y_far, z_next, z_last, far, mate)
    for peer in everyone:
        pl.semaphore_signal(barrier, inc=1, device_id=peer, device_id_type=pl.DeviceIdType.MESH)

    node = (x + x // 2) % 2 + 2 * (x // 2) + 4 * zl

    def home(rank):
        return (zh - rank // 4) % 2 * 4 + (y - rank % 4) % 4

    def remote(src, dst, send, recv, peer):
        return pltpu.make_async_remote_copy(
            src_ref=src, dst_ref=dst, send_sem=send, recv_sem=recv,
            device_id=peer, device_id_type=pl.DeviceIdType.MESH)

    class Near:
        def __init__(self, buf, total, y0, plane, first, stride, stage, recv, send):
            self.buf, self.total, self.recv, self.send = buf, total, recv, send
            self.first, self.stride, self.stage = first, stride, stage
            dy = (y - y0) % 4
            self.mine = core == plane
            self.depth = (jnp.where(z == 0, 0, 1) + jnp.where(x == 0, 0, 1) + jnp.where(dy == 0, 0, 1))
            on_z = (z == 0) & (x == 0) & (dy == 0) & self.mine
            on_x = (x == 0) & (dy == 0) & self.mine
            on_y = (dy == 0) & self.mine
            self.peers = (z_next, z_last, far, x_next, x_last, x_far, y_next, y_last, y_far, mate)
            self.groups = ((on_z, (0, 1, 2)), (on_x, (3, 4, 5)), (on_y, (6, 7, 8)))
            self.on_y = on_y
            self.units = first + (total - 1) * stride + 3 * stage + 2

        def copy(self, n, way):
            return remote(self.buf.at[n], self.buf.at[n], self.send.at[n, way], self.recv.at[n], self.peers[way])

        def step(self, unit):
            since = unit - self.first - self.stage * self.depth - jnp.where(self.mine, 0, 1)
            n = since // self.stride

            @pl.when((since >= 0) & (since % self.stride == 0) & (n < self.total))
            def _():
                @pl.when((self.depth > 0) | jnp.logical_not(self.mine))
                def _():
                    self.copy(n, 0).wait_recv()

                @pl.when(self.mine)
                def _():
                    @pl.when(self.on_y)
                    def _():
                        for cond, ways in self.groups:
                            @pl.when(cond)
                            def _():
                                for way in ways:
                                    self.copy(n, way).start()
                    self.copy(n, 9).start()

        def end(self):
            for cond, ways in self.groups + ((self.mine, (9,)),):
                @pl.when(cond)
                def _():
                    for way in ways:
                        for n in range(self.total):
                            self.copy(n, way).wait_send()

    near0 = Near(a00, 5, 0, 0, 0, 1, 3, d0_recv, d0_send)
    near1 = Near(a10, 8, 1, 0, 2, 2, 5, d1_recv, d1_send)
    near2 = Near(a11, 5, 1, 1, 2, 2, 5, d2_recv, d2_send)

    here = lax.broadcasted_iota(jnp.int32, (B, B), 0)
    there = lax.broadcasted_iota(jnp.int32, (B, B), 1)

    def put_upper(buf):
        a = stage[0]
        a = (0.5 * (a + a.T) - jnp.where(here == there, SHIFT, 0.0)).astype(BF16)
        for e, (i, j) in enumerate(UPPER):
            buf[e // 2, e % 2] = a[128 * i:128 * i + 128, 128 * j:128 * j + 128]

    @pl.when(root)
    def _():
        load(0).wait()
        for s in range(1, SLOTS):
            load(s).start()

    @pl.when((rank_row == 0) & (rank_col == 0))
    def _():
        put_upper(a00)

    @pl.when((rank_row == 1) & (rank_col == 1))
    def _():
        put_upper(a11)

    @pl.when((rank_row == 1) & (rank_col == 0))
    def _():
        for q in range(8):
            a10[q] = stage[0, q * 64:(q + 1) * 64, :].astype(BF16)

    pl.semaphore_wait(barrier, len(everyone))

    def row_copy(t, n, d):
        block = rows.at[core, t + (SECOND[t] - t) * (n // Q), n % Q]
        return remote(block, block, row_send.at[t, n, d], row_recv.at[t, n], row_peers[d])

    def mate_copy(t, n, panel):
        block = rows.at[panel, t + (SECOND[t] - t) * (n // Q), n % Q]
        return remote(block, block, mate_send.at[t, n], mate_recv.at[t, n], mate)

    def col_copy(p, n, d):
        block = cols.at[p, n // Q, n % Q]
        return remote(block, block, col_send.at[p, n, d], col_recv.at[p, n], col_peers[d])

    col_node = home(rank_col % 8)
    row_depth = [lookup(ROW_TREES[t][0], node) for t in range(3)]
    row_child = [[member(ROW_TREES[t][1][d], node) for d in range(3)] for t in range(3)]
    even = core == 0
    col_depth = [jnp.where(even, lookup(COL_TREES[0][p][0], col_node), lookup(COL_TREES[1][p][0], col_node))
                 for p in range(2)]
    col_child = [[(even & member(COL_TREES[0][p][1][d], col_node))
                  | (jnp.logical_not(even) & member(COL_TREES[1][p][1][d], col_node)) for d in range(3)]
                 for p in range(2)]

    def bulk(h):
        if h < N_ROW:
            q = h % Q
            for t in range(3):
                slot = SECOND[t] if h >= Q else t

                @pl.when(root)
                def _():
                    if q == 0 and slot > 0:
                        load(slot).wait()
                    rows[core, slot, q] = stage[slot, q * QR:(q + 1) * QR, :].astype(BF16)

        for t in range(3):
            if h < ROW_STEPS:
                n = h - LAG * row_depth[t]

                @pl.when((n >= 0) & (n < N_ROW))
                def _():
                    @pl.when(row_depth[t] > 0)
                    def _():
                        row_copy(t, n, 0).wait_recv()
                    for d in range(3):
                        @pl.when(row_child[t][d])
                        def _():
                            row_copy(t, n, d).start()
                    mate_copy(t, n, core).start()
                before = n - 1

                @pl.when((before >= 0) & (before < N_ROW))
                def _():
                    mate_copy(t, before, flip(core)).wait_recv()

        if h >= COL_START:
            for p in range(2):
                n = h - COL_START - LAG * col_depth[p]

                @pl.when((n >= 0) & (n < N_COL))
                def _():
                    @pl.when(col_depth[p] == 0)
                    def _():
                        cols[p, n // Q, n % Q] = rows[p, rank_col // 8 + 2 * (n // Q), n % Q]

                    @pl.when(col_depth[p] > 0)
                    def _():
                        col_copy(p, n, 0).wait_recv()
                    for d in range(3):
                        @pl.when(col_child[p][d])
                        def _():
                            col_copy(p, n, d).start()

    count = {"hook": 0, "unit": 0, "bulk": 0}
    nears = (near0, near1, near2)
    units = max(near.units for near in nears)

    def next_unit():
        unit = count["unit"]
        if unit < units:
            for near in nears:
                if near.first <= unit < near.units:
                    near.step(unit)
            count["unit"] += 1

    def next_bulk():
        if count["bulk"] < STEPS:
            bulk(count["bulk"])
            count["bulk"] += 1

    def hook():
        done = count["hook"]
        count["hook"] += 1
        while count["unit"] < min(units, FIRST_UNITS + (done + 1) * (units - FIRST_UNITS) // HOOKS):
            next_unit()
        if count["hook"] % BULK_HOOKS == 0:
            next_bulk()

    while count["unit"] < FIRST_UNITS:
        next_unit()
        if count["unit"] % 2:
            next_bulk()

    def used(panel, i):
        return jnp.where(i > panel, pattern[panel, i], 0)

    def begin(get, blocks):
        for i, j in blocks:
            block = get(i, j)
            if i == j:
                block = block + jnp.where(here[:128, :128] == there[:128, :128], SHIFT, 0.0)
            M[128 * i:128 * i + 128, 128 * j:128 * j + 128] = block

    def finish(U, w):
        for k in range(1, 4):
            U[128 * k:128 * k + 128, 0:128 * k] = jnp.zeros((128, 128 * k), F32)
        W[w] = M[:, B:2 * B].astype(BF16)

    def first(i, j):
        e = UPPER.index((i, j))
        return a00[e // 2, e % 2].astype(F32)

    M[:, B:2 * B] = jnp.zeros((B, B), F32)
    begin(first, UPPER[:1])
    factor_tile(M, U0, W128, hook, lambda: begin(first, UPPER[1:]))
    finish(U0, 0)
    while count["unit"] < units:
        next_unit()
    lead = (used(0, 1).astype(F32) * dot1(a10[...].reshape(B, B), W[0], NT)).astype(BF16)
    L1[...] = lead

    def second(i, j):
        e = UPPER.index((i, j))
        return a11[e // 2, e % 2].astype(F32) - dot1(
            L1[128 * i:128 * i + 128, :], L1[128 * j:128 * j + 128, :], NT)

    M[:, B:2 * B] = jnp.zeros((B, B), F32)
    begin(second, UPPER)
    factor_tile(M, U1, W128, hook, lambda: None)
    finish(U1, 1)

    ends = [
        pltpu.make_async_copy(U0, F_out.at[0], out_sem.at[0]),
        pltpu.make_async_copy(U1, F_out.at[1], out_sem.at[1]),
        pltpu.make_async_copy(W, W_out, out_sem.at[2]),
        pltpu.make_async_copy(L1, L_out, out_sem.at[3]),
    ]
    for end in ends:
        end.start()

    def solve_row(slot):
        i = rank_row + 8 * slot
        first_b = (used(0, i).astype(F32) * dot1(rows[0, slot].reshape(B, B), W[0], NT)).astype(BF16)
        left = rows[1, slot].reshape(B, B).astype(F32) - dot1(first_b, L1[...], NT)
        solved[0, slot] = first_b
        solved[1, slot] = (used(1, i).astype(F32) * dot1(left.astype(BF16), W[1], NT)).astype(BF16)
        end = pltpu.make_async_copy(solved.at[:, slot], rows_out.at[:, slot], row_out_sem.at[slot])
        end.start()
        ends.append(end)

    while count["bulk"] < ROW_STEPS:
        next_bulk()
    for slot in range(SLOTS):
        if slot % 2 == 0:
            next_bulk()
        solve_row(slot)
    while count["bulk"] < STEPS:
        next_bulk()
    ends.append(pltpu.make_async_copy(cols, cols_out, out_sem.at[4]))
    ends[-1].start()

    for t in range(3):
        for d in range(3):
            if ROW_TREES[t][1][d]:
                @pl.when(row_child[t][d])
                def _():
                    for n in range(N_ROW):
                        row_copy(t, n, d).wait_send()
        for n in range(N_ROW):
            mate_copy(t, n, core).wait_send()
    for p in range(2):
        for d in range(3):
            @pl.when(col_child[p][d])
            def _():
                for n in range(N_COL):
                    col_copy(p, n, d).wait_send()
    for near in nears:
        near.end()
    for end in ends:
        end.wait()


def front(pattern, tiles):
    hbm = pl.BlockSpec(memory_space=pl.ANY)
    dma = pltpu.SemaphoreType.DMA
    return pl.pallas_call(
        front_kernel,
        out_shape=[
            jax.ShapeDtypeStruct((2, SLOTS, B, B), BF16),
            jax.ShapeDtypeStruct((2, 2, Q, QR, B), BF16),
            jax.ShapeDtypeStruct((2, B, B), F32),
            jax.ShapeDtypeStruct((2, B, B), BF16),
            jax.ShapeDtypeStruct((B, B), BF16),
        ],
        in_specs=[pl.BlockSpec(memory_space=pltpu.SMEM), hbm],
        out_specs=[hbm] * 5,
        scratch_shapes=[
            pltpu.VMEM((2, SLOTS, Q, QR, B), BF16),
            pltpu.VMEM((2, 2, Q, QR, B), BF16),
            pltpu.VMEM((2, SLOTS, B, B), BF16),
            pltpu.VMEM((SLOTS, B, B), F32),
            pltpu.VMEM((5, 2, 128, 128), BF16),
            pltpu.VMEM((8, 64, B), BF16),
            pltpu.VMEM((5, 2, 128, 128), BF16),
            pltpu.VMEM((B, 2 * B), F32),
            pltpu.VMEM((B, B), F32),
            pltpu.VMEM((B, B), F32),
            pltpu.VMEM((128, 128), F32),
            pltpu.VMEM((2, B, B), BF16),
            pltpu.VMEM((B, B), BF16),
            dma((SLOTS,)),
            dma((5,)),
            dma((SLOTS,)),
            dma((3, N_ROW)),
            dma((3, N_ROW, 3)),
            dma((3, N_ROW)),
            dma((3, N_ROW)),
            dma((2, N_COL)),
            dma((2, N_COL, 3)),
            dma((5,)),
            dma((5, 10)),
            dma((8,)),
            dma((8, 10)),
            dma((5,)),
            dma((5, 10)),
        ],
        compiler_params=pltpu.CompilerParams(
            collective_id=0, has_side_effects=True, vmem_limit_bytes=48 << 20),
        name="front",
    )(pattern, tiles)


def halves(a):
    high = a.astype(BF16)
    return high, (a - high.astype(F32)).astype(BF16)


def dot1(a, b, dims):
    return lax.dot_general(a, b, (dims, ((), ())), preferred_element_type=F32)


def dot3(a, b, dims):
    ah, al = halves(a)
    bh, bl = halves(b)
    return dot1(ah, bh, dims) + (dot1(ah, bl, dims) + dot1(al, bh, dims))


NN = ((1,), (0,))
TN = ((0,), (0,))
NT = ((1,), (1,))


def factor128(S, hook):
    lane = lax.broadcasted_iota(jnp.int32, (8, 128), 1)
    sub = lax.broadcasted_iota(jnp.int32, (8, 128), 0)
    T = [jnp.where(lane == sub + 8 * h, 1.0, 0.0).astype(F32) for h in range(16)]
    S = list(S)
    upper, inverse = [], []

    def along(v, l):
        return jnp.broadcast_to(v[:, l:l + 1], (8, 128))

    def down(v, s):
        return jnp.broadcast_to(v[s:s + 1, :], (8, 128))

    for g in range(16):
        p = 8 * g
        multipliers = [[along(S[h], p + s) for s in range(8)] for h in range(g, 16)]
        c = list(multipliers[0])
        X, Y = S[g], T[g]
        RX = jnp.zeros((8, 128), F32)
        RY = RX
        for s in range(8):
            root = lax.rsqrt(down(c[s], s))
            inv = root * root
            xr, yr = down(X, s), down(Y, s)
            me = sub == s
            RX = jnp.where(me, xr * root, RX)
            RY = jnp.where(me, yr * root, RY)
            qx, qy = xr * inv, yr * inv
            X = jnp.where(me, qx, X - c[s] * qx)
            Y = jnp.where(me, qy, Y - c[s] * qy)
            for u in range(s + 1, 8):
                qc = down(c[u], s) * inv
                c[u] = jnp.where(me, qc, c[u] - c[s] * qc)
        upper.append(RX)
        inverse.append(RY)
        if g in HOOK_GROUPS:
            hook()
        if g < 15:
            QX = [down(X, s) for s in range(8)]
            QY = [down(Y, s) for s in range(8)]
            for h in range(g + 1, 16):
                a, t = S[h], T[h]
                for s in range(8):
                    m = multipliers[h - g][s]
                    a = a - m * QX[s]
                    t = t - m * QY[s]
                S[h], T[h] = a, t
    return upper, inverse


def factor_tile(M, U, W128, hook, rest):
    for k in range(4):
        b = 128 * k
        upper, inverse = factor128([M[b + 8 * h:b + 8 * h + 8, b:b + 128] for h in range(16)], hook)
        if k == 0:
            rest()
        lane = lax.broadcasted_iota(jnp.int32, (8, 128), 1)
        sub = lax.broadcasted_iota(jnp.int32, (8, 128), 0)
        for h in range(16):
            U[b + 8 * h:b + 8 * h + 8, b:b + 128] = jnp.where(lane >= sub + 8 * h, upper[h], 0.0)
            W128[8 * h:8 * h + 8, :] = jnp.where(lane <= sub + 8 * h, inverse[h], 0.0)
        block = W128[...]
        M[b:b + 128, 512 + b:640 + b] = block
        R = dot3(block, M[b:b + 128, b + 128:b + 512], NN)
        M[b:b + 128, b + 128:b + 512] = R
        if k < 3:
            n = 384 - 128 * k
            U[b:b + 128, b + 128:512] = R[:, :n]
            wide = M[b:b + 128, b + 128:b + 640]
            for r in range(k + 1, 4):
                o = 128 * (r - k - 1)
                M[128 * r:128 * r + 128, b + 128:b + 640] -= dot3(R[:, o:o + 128], wide, TN)


def update_kernel(pattern, tiles, rows_in, cols_in, F_in, W_in, L_in, out, rows, cols, F, W, L1, work, sems, row_sem, tile_sem, out_sem):
    rank_row = lax.axis_index("row")
    rank_col = lax.axis_index("col")

    early = [
        pltpu.make_async_copy(W_in, W, sems.at[0]),
        pltpu.make_async_copy(L_in, L1, sems.at[1]),
        pltpu.make_async_copy(cols_in, cols, sems.at[2]),
    ]
    F_copy = pltpu.make_async_copy(F_in.at[jnp.minimum(rank_col, 1)], F, sems.at[3])

    def row_load(s):
        return pltpu.make_async_copy(rows_in.at[:, s], rows.at[:, s], row_sem.at[s])

    def tile_load(s):
        return pltpu.make_async_copy(tiles.at[s], work.at[s], tile_sem.at[s])

    for load in early:
        load.start()
    for s in range(SLOTS):
        row_load(s).start()
        tile_load(s).start()
        if s == 0:
            @pl.when((rank_row == rank_col) & (rank_col < 2))
            def _():
                F_copy.start()

    def used(panel, i):
        return jnp.where(i > panel, pattern[panel, i], 0)

    def solve(a, w):
        return dot1(a, W[w], NT)

    for load in early:
        load.wait()

    for k in range(2):
        j = rank_col + 16 * k

        @pl.when(used(0, j) > 0)
        def _():
            cols[0, k] = solve(cols[0, k], 0).astype(BF16)

        @pl.when(used(1, j) > 0)
        def _():
            @pl.when(used(0, j) > 0)
            def _():
                cols[1, k] = (cols[1, k].astype(F32) - dot1(cols[0, k], L1[...], NT)).astype(BF16)
            cols[1, k] = solve(cols[1, k], 1).astype(BF16)

    def one_row(s, carry):
        i = rank_row + 8 * s
        row_load(s).wait()
        tile_load(s).wait()

        @pl.when((rank_col < 2) & (i > rank_col))
        def _():
            work[s, 0] = rows[jnp.minimum(rank_col, 1), s].astype(F32)

        for k in range(2):
            j = rank_col + 16 * k
            for p in range(2):
                on = (j > 1) & (i >= j) & (used(p, i) > 0) & (used(p, j) > 0)

                @pl.when(on)
                def _():
                    work[s, k] -= dot1(rows[p, s], cols[p, k], NT)

        @pl.when((s == 0) & (rank_row == rank_col) & (rank_col < 2))
        def _():
            F_copy.wait()
            work[0, 0] = F[...].T

        pltpu.make_async_copy(work.at[s], out.at[s], out_sem.at[s]).start()
        return carry

    lax.fori_loop(0, SLOTS, one_row, 0)
    for s in range(SLOTS):
        pltpu.make_async_copy(work.at[s], out.at[s], out_sem.at[s]).wait()


def update(pattern, tiles, *found):
    hbm = pl.BlockSpec(memory_space=pl.ANY)
    return pl.pallas_call(
        update_kernel,
        out_shape=jax.ShapeDtypeStruct(tiles.shape, F32),
        in_specs=[pl.BlockSpec(memory_space=pltpu.SMEM)] + [hbm] * 6,
        out_specs=hbm,
        scratch_shapes=[
            pltpu.VMEM((2, SLOTS, B, B), BF16),
            pltpu.VMEM((2, 2, B, B), BF16),
            pltpu.VMEM((B, B), F32),
            pltpu.VMEM((2, B, B), BF16),
            pltpu.VMEM((B, B), BF16),
            pltpu.VMEM((SLOTS, 2, B, B), F32),
            pltpu.SemaphoreType.DMA((4,)),
            pltpu.SemaphoreType.DMA((SLOTS,)),
            pltpu.SemaphoreType.DMA((SLOTS,)),
            pltpu.SemaphoreType.DMA((SLOTS,)),
        ],
        compiler_params=pltpu.CompilerParams(vmem_limit_bytes=48 << 20),
        name="update",
    )(pattern, tiles, *found)


def per_device(tiles, pattern):
    rows, cols, factors, inverses, lead = front(pattern, tiles)
    return update(
        pattern, tiles, rows, cols.reshape(2, 2, B, B), factors, inverses, lead)


def solution(mesh):
    placed = P("row", "col", None, None)
    return jax.shard_map(
        per_device,
        mesh=mesh,
        in_specs=(placed, P()),
        out_specs=placed,
        check_vma=False,
    )
```

```python
import jax
import jax.numpy as jnp
from jax import lax
from jax.experimental import pallas as pl
from jax.experimental.pallas import tpu as pltpu
from jax.sharding import PartitionSpec as P

F32 = jnp.float32
BF16 = jnp.bfloat16
B = 512
SLOTS = 6
Q = 4
QR = B // Q
SHIFT = 128.0


def flip(bit):
    return 1 - bit


def lookup(table, index):
    total = jnp.int32(0)
    for value, entry in enumerate(table):
        if entry:
            total = total + jnp.where(index == value, entry, 0)
    return total


def member(values, index):
    hit = jnp.bool_(False)
    for value in values:
        hit = hit | (index == value)
    return hit


def row_tree(t):
    depth = {0: 0, 1 << t: 1}
    children = {0: [], 1: [], 2: []}
    children[t].append(0)
    for d in ((t + 1) % 3, (t + 2) % 3, t):
        for node in list(depth):
            other = node ^ (1 << d)
            if node != 0 and other not in depth:
                depth[other] = depth[node] + 1
                children[d].append(node)
    return [depth[v] for v in range(8)], [children[d] for d in range(3)]


def column_tree(sign, cross):
    depth = [0] * 8
    children = [[], [], []]
    ahead, behind = (0, 1) if sign > 0 else (1, 0)

    def ring(z, start, base):
        children[ahead].append(z * 4 + start)
        first = (start + sign) % 4
        depth[z * 4 + first] = base + 1
        children[ahead].append(z * 4 + first)
        depth[z * 4 + (first + sign) % 4] = base + 2
        children[behind].append(z * 4 + start)
        depth[z * 4 + (start - sign) % 4] = base + 1

    ring(0, 0, 0)
    children[2].append(cross)
    depth[4 + cross] = depth[cross] + 1
    ring(1, cross, depth[cross] + 1)
    return depth, children


ROW_TREES = [row_tree(t) for t in range(3)]
COL_TREES = [[column_tree(sign, 0), column_tree(sign, sign % 4)] for sign in (-1, 1)]
N_ROW = 2 * Q
N_COL = 2 * Q
LAG = 2
COL_START = 3 * LAG + 1
SECOND = (4, 3, 5)
ROW_STEPS = N_ROW + 4 * LAG + 1
STEPS = COL_START + N_COL + 4 * LAG
UPPER = [(i, j) for i in range(4) for j in range(i, 4)]
HOOK_GROUPS = (1, 3, 5, 7, 9, 11, 13, 15)
HOOKS = 4 * len(HOOK_GROUPS)
FIRST_UNITS = 11
BULK_HOOKS = 5


def front_kernel(pattern, tiles, rows_out, cols_out, F_out, W_out, L_out,
                 rows, cols, solved, stage, a00, a10, a11, M, U0, U1, W128, W, L1,
                 load_sem, out_sem, row_out_sem, row_recv, row_send, mate_recv, mate_send, col_recv, col_send,
                 d0_recv, d0_send, d1_recv, d1_send, d2_recv, d2_send):
    rank_row = lax.axis_index("row")
    rank_col = lax.axis_index("col")
    zh, y = rank_row // 4, rank_row % 4
    x, zl, core = rank_col // 4, (rank_col // 2) % 2, rank_col % 2
    z = zh * 2 + zl
    root = rank_col < 2

    def at(x1, y1, z1, core1):
        return ((z1 // 2) * 4 + y1, x1 * 4 + (z1 % 2) * 2 + core1)

    x_next, x_last = at((x + 1) % 4, y, z, core), at((x + 3) % 4, y, z, core)
    y_next, y_last = at(x, (y + 1) % 4, z, core), at(x, (y + 3) % 4, z, core)
    z_next, z_last = at(x, y, (z + 1) % 4, core), at(x, y, (z + 3) % 4, core)
    mate = at(x, y, z, flip(core))
    far = at(x, y, (z + 2) % 4, core)
    x_far, y_far = at((x + 2) % 4, y, z, core), at(x, (y + 2) % 4, z, core)
    row_peers = (
        at(x + 1 - 2 * (x % 2), y, z, core),
        at(3 - x, y, z, core),
        at(x, y, z + 1 - 2 * zl, core),
    )
    col_peers = (y_next, y_last, far)

    def load(s):
        return pltpu.make_async_copy(tiles.at[s, 0], stage.at[s], load_sem.at[s])

    @pl.when(root)
    def _():
        load(0).start()

    barrier = pltpu.get_barrier_semaphore()
    everyone = (x_next, x_last, x_far, y_next, y_last, y_far, z_next, z_last, far, mate)
    for peer in everyone:
        pl.semaphore_signal(barrier, inc=1, device_id=peer, device_id_type=pl.DeviceIdType.MESH)

    node = (x + x // 2) % 2 + 2 * (x // 2) + 4 * zl

    def home(rank):
        return (zh - rank // 4) % 2 * 4 + (y - rank % 4) % 4

    def remote(src, dst, send, recv, peer):
        return pltpu.make_async_remote_copy(
            src_ref=src, dst_ref=dst, send_sem=send, recv_sem=recv,
            device_id=peer, device_id_type=pl.DeviceIdType.MESH)

    class Near:
        def __init__(self, buf, total, y0, plane, first, stride, stage, recv, send):
            self.buf, self.total, self.recv, self.send = buf, total, recv, send
            self.first, self.stride, self.stage = first, stride, stage
            dy = (y - y0) % 4
            self.mine = core == plane
            self.depth = (jnp.where(z == 0, 0, 1) + jnp.where(x == 0, 0, 1) + jnp.where(dy == 0, 0, 1))
            on_z = (z == 0) & (x == 0) & (dy == 0) & self.mine
            on_x = (x == 0) & (dy == 0) & self.mine
            on_y = (dy == 0) & self.mine
            self.peers = (z_next, z_last, far, x_next, x_last, x_far, y_next, y_last, y_far, mate)
            self.groups = ((on_z, (0, 1, 2)), (on_x, (3, 4, 5)), (on_y, (6, 7, 8)))
            self.on_y = on_y
            self.units = first + (total - 1) * stride + 3 * stage + 2

        def copy(self, n, way):
            return remote(self.buf.at[n], self.buf.at[n], self.send.at[n, way], self.recv.at[n], self.peers[way])

        def step(self, unit):
            since = unit - self.first - self.stage * self.depth - jnp.where(self.mine, 0, 1)
            n = since // self.stride

            @pl.when((since >= 0) & (since % self.stride == 0) & (n < self.total))
            def _():
                @pl.when((self.depth > 0) | jnp.logical_not(self.mine))
                def _():
                    self.copy(n, 0).wait_recv()

                @pl.when(self.mine)
                def _():
                    @pl.when(self.on_y)
                    def _():
                        for cond, ways in self.groups:
                            @pl.when(cond)
                            def _():
                                for way in ways:
                                    self.copy(n, way).start()
                    self.copy(n, 9).start()

        def end(self):
            for cond, ways in self.groups + ((self.mine, (9,)),):
                @pl.when(cond)
                def _():
                    for way in ways:
                        for n in range(self.total):
                            self.copy(n, way).wait_send()

    near0 = Near(a00, 5, 0, 0, 0, 1, 3, d0_recv, d0_send)
    near1 = Near(a10, 8, 1, 0, 2, 2, 5, d1_recv, d1_send)
    near2 = Near(a11, 5, 1, 1, 2, 2, 5, d2_recv, d2_send)

    here = lax.broadcasted_iota(jnp.int32, (B, B), 0)
    there = lax.broadcasted_iota(jnp.int32, (B, B), 1)

    def put_upper(buf):
        a = stage[0]
        a = (0.5 * (a + a.T) - jnp.where(here == there, SHIFT, 0.0)).astype(BF16)
        for e, (i, j) in enumerate(UPPER):
            buf[e // 2, e % 2] = a[128 * i:128 * i + 128, 128 * j:128 * j + 128]

    @pl.when(root)
    def _():
        load(0).wait()
        for s in range(1, SLOTS):
            load(s).start()

    @pl.when((rank_row == 0) & (rank_col == 0))
    def _():
        put_upper(a00)

    @pl.when((rank_row == 1) & (rank_col == 1))
    def _():
        put_upper(a11)

    @pl.when((rank_row == 1) & (rank_col == 0))
    def _():
        for q in range(8):
            a10[q] = stage[0, q * 64:(q + 1) * 64, :].astype(BF16)

    pl.semaphore_wait(barrier, len(everyone))

    def row_copy(t, n, d):
        block = rows.at[core, t + (SECOND[t] - t) * (n // Q), n % Q]
        return remote(block, block, row_send.at[t, n, d], row_recv.at[t, n], row_peers[d])

    def mate_copy(t, n, panel):
        block = rows.at[panel, t + (SECOND[t] - t) * (n // Q), n % Q]
        return remote(block, block, mate_send.at[t, n], mate_recv.at[t, n], mate)

    def col_copy(p, n, d):
        block = cols.at[p, n // Q, n % Q]
        return remote(block, block, col_send.at[p, n, d], col_recv.at[p, n], col_peers[d])

    col_node = home(rank_col % 8)
    row_depth = [lookup(ROW_TREES[t][0], node) for t in range(3)]
    row_child = [[member(ROW_TREES[t][1][d], node) for d in range(3)] for t in range(3)]
    even = core == 0
    col_depth = [jnp.where(even, lookup(COL_TREES[0][p][0], col_node), lookup(COL_TREES[1][p][0], col_node))
                 for p in range(2)]
    col_child = [[(even & member(COL_TREES[0][p][1][d], col_node))
                  | (jnp.logical_not(even) & member(COL_TREES[1][p][1][d], col_node)) for d in range(3)]
                 for p in range(2)]

    def bulk(h):
        if h < N_ROW:
            q = h % Q
            for t in range(3):
                slot = SECOND[t] if h >= Q else t

                @pl.when(root)
                def _():
                    if q == 0 and slot > 0:
                        load(slot).wait()
                    rows[core, slot, q] = stage[slot, q * QR:(q + 1) * QR, :].astype(BF16)

        for t in range(3):
            if h < ROW_STEPS:
                n = h - LAG * row_depth[t]

                @pl.when((n >= 0) & (n < N_ROW))
                def _():
                    @pl.when(row_depth[t] > 0)
                    def _():
                        row_copy(t, n, 0).wait_recv()
                    for d in range(3):
                        @pl.when(row_child[t][d])
                        def _():
                            row_copy(t, n, d).start()
                    mate_copy(t, n, core).start()
                before = n - 1

                @pl.when((before >= 0) & (before < N_ROW))
                def _():
                    mate_copy(t, before, flip(core)).wait_recv()

        if h >= COL_START:
            for p in range(2):
                n = h - COL_START - LAG * col_depth[p]

                @pl.when((n >= 0) & (n < N_COL))
                def _():
                    @pl.when(col_depth[p] == 0)
                    def _():
                        cols[p, n // Q, n % Q] = rows[p, rank_col // 8 + 2 * (n // Q), n % Q]

                    @pl.when(col_depth[p] > 0)
                    def _():
                        col_copy(p, n, 0).wait_recv()
                    for d in range(3):
                        @pl.when(col_child[p][d])
                        def _():
                            col_copy(p, n, d).start()

    count = {"hook": 0, "unit": 0, "bulk": 0}
    nears = (near0, near1, near2)
    units = max(near.units for near in nears)

    def next_unit():
        unit = count["unit"]
        if unit < units:
            for near in nears:
                if near.first <= unit < near.units:
                    near.step(unit)
            count["unit"] += 1

    def next_bulk():
        if count["bulk"] < STEPS:
            bulk(count["bulk"])
            count["bulk"] += 1

    def hook():
        done = count["hook"]
        count["hook"] += 1
        while count["unit"] < min(units, FIRST_UNITS + (done + 1) * (units - FIRST_UNITS) // HOOKS):
            next_unit()
        if count["hook"] % BULK_HOOKS == 0:
            next_bulk()

    while count["unit"] < FIRST_UNITS:
        next_unit()
        if count["unit"] % 2:
            next_bulk()

    def used(panel, i):
        return jnp.where(i > panel, pattern[panel, i], 0)

    def begin(get, blocks):
        for i, j in blocks:
            block = get(i, j)
            if i == j:
                block = block + jnp.where(here[:128, :128] == there[:128, :128], SHIFT, 0.0)
            M[128 * i:128 * i + 128, 128 * j:128 * j + 128] = block

    def finish(U, w):
        for k in range(1, 4):
            U[128 * k:128 * k + 128, 0:128 * k] = jnp.zeros((128, 128 * k), F32)
        W[w] = M[:, B:2 * B].astype(BF16)

    def first(i, j):
        e = UPPER.index((i, j))
        return a00[e // 2, e % 2].astype(F32)

    M[:, B:2 * B] = jnp.zeros((B, B), F32)
    begin(first, UPPER[:1])
    factor_tile(M, U0, W128, hook, lambda: begin(first, UPPER[1:]))
    finish(U0, 0)
    while count["unit"] < units:
        next_unit()
    lead = (used(0, 1).astype(F32) * dot1(a10[...].reshape(B, B), W[0], NT)).astype(BF16)
    L1[...] = lead

    def second(i, j):
        e = UPPER.index((i, j))
        return a11[e // 2, e % 2].astype(F32) - dot1(
            L1[128 * i:128 * i + 128, :], L1[128 * j:128 * j + 128, :], NT)

    M[:, B:2 * B] = jnp.zeros((B, B), F32)
    begin(second, UPPER)
    factor_tile(M, U1, W128, hook, lambda: None)
    finish(U1, 1)

    ends = [
        pltpu.make_async_copy(U0, F_out.at[0], out_sem.at[0]),
        pltpu.make_async_copy(U1, F_out.at[1], out_sem.at[1]),
        pltpu.make_async_copy(W, W_out, out_sem.at[2]),
        pltpu.make_async_copy(L1, L_out, out_sem.at[3]),
    ]
    for end in ends:
        end.start()

    def solve_row(slot):
        i = rank_row + 8 * slot
        first_b = (used(0, i).astype(F32) * dot1(rows[0, slot].reshape(B, B), W[0], NT)).astype(BF16)
        left = rows[1, slot].reshape(B, B).astype(F32) - dot1(first_b, L1[...], NT)
        solved[0, slot] = first_b
        solved[1, slot] = (used(1, i).astype(F32) * dot1(left.astype(BF16), W[1], NT)).astype(BF16)
        end = pltpu.make_async_copy(solved.at[:, slot], rows_out.at[:, slot], row_out_sem.at[slot])
        end.start()
        ends.append(end)

    while count["bulk"] < ROW_STEPS:
        next_bulk()
    for slot in range(SLOTS):
        if slot % 2 == 0:
            next_bulk()
        solve_row(slot)
    while count["bulk"] < STEPS:
        next_bulk()
    ends.append(pltpu.make_async_copy(cols, cols_out, out_sem.at[4]))
    ends[-1].start()

    for t in range(3):
        for d in range(3):
            if ROW_TREES[t][1][d]:
                @pl.when(row_child[t][d])
                def _():
                    for n in range(N_ROW):
                        row_copy(t, n, d).wait_send()
        for n in range(N_ROW):
            mate_copy(t, n, core).wait_send()
    for p in range(2):
        for d in range(3):
            @pl.when(col_child[p][d])
            def _():
                for n in range(N_COL):
                    col_copy(p, n, d).wait_send()
    for near in nears:
        near.end()
    for end in ends:
        end.wait()


def front(pattern, tiles):
    hbm = pl.BlockSpec(memory_space=pl.ANY)
    dma = pltpu.SemaphoreType.DMA
    return pl.pallas_call(
        front_kernel,
        out_shape=[
            jax.ShapeDtypeStruct((2, SLOTS, B, B), BF16),
            jax.ShapeDtypeStruct((2, 2, Q, QR, B), BF16),
            jax.ShapeDtypeStruct((2, B, B), F32),
            jax.ShapeDtypeStruct((2, B, B), BF16),
            jax.ShapeDtypeStruct((B, B), BF16),
        ],
        in_specs=[pl.BlockSpec(memory_space=pltpu.SMEM), hbm],
        out_specs=[hbm] * 5,
        scratch_shapes=[
            pltpu.VMEM((2, SLOTS, Q, QR, B), BF16),
            pltpu.VMEM((2, 2, Q, QR, B), BF16),
            pltpu.VMEM((2, SLOTS, B, B), BF16),
            pltpu.VMEM((SLOTS, B, B), F32),
            pltpu.VMEM((5, 2, 128, 128), BF16),
            pltpu.VMEM((8, 64, B), BF16),
            pltpu.VMEM((5, 2, 128, 128), BF16),
            pltpu.VMEM((B, 2 * B), F32),
            pltpu.VMEM((B, B), F32),
            pltpu.VMEM((B, B), F32),
            pltpu.VMEM((128, 128), F32),
            pltpu.VMEM((2, B, B), BF16),
            pltpu.VMEM((B, B), BF16),
            dma((SLOTS,)),
            dma((5,)),
            dma((SLOTS,)),
            dma((3, N_ROW)),
            dma((3, N_ROW, 3)),
            dma((3, N_ROW)),
            dma((3, N_ROW)),
            dma((2, N_COL)),
            dma((2, N_COL, 3)),
            dma((5,)),
            dma((5, 10)),
            dma((8,)),
            dma((8, 10)),
            dma((5,)),
            dma((5, 10)),
        ],
        compiler_params=pltpu.CompilerParams(
            collective_id=0, has_side_effects=True, vmem_limit_bytes=48 << 20),
        name="front",
    )(pattern, tiles)


def halves(a):
    high = a.astype(BF16)
    return high, (a - high.astype(F32)).astype(BF16)


def dot1(a, b, dims):
    return lax.dot_general(a, b, (dims, ((), ())), preferred_element_type=F32)


def dot3(a, b, dims):
    ah, al = halves(a)
    bh, bl = halves(b)
    return dot1(ah, bh, dims) + (dot1(ah, bl, dims) + dot1(al, bh, dims))


NN = ((1,), (0,))
TN = ((0,), (0,))
NT = ((1,), (1,))


def factor128(S, hook):
    lane = lax.broadcasted_iota(jnp.int32, (8, 128), 1)
    sub = lax.broadcasted_iota(jnp.int32, (8, 128), 0)
    T = [jnp.where(lane == sub + 8 * h, 1.0, 0.0).astype(F32) for h in range(16)]
    S = list(S)
    upper, inverse = [], []

    def along(v, l):
        return jnp.broadcast_to(v[:, l:l + 1], (8, 128))

    def down(v, s):
        return jnp.broadcast_to(v[s:s + 1, :], (8, 128))

    for g in range(16):
        p = 8 * g
        multipliers = [[along(S[h], p + s) for s in range(8)] for h in range(g, 16)]
        c = list(multipliers[0])
        X, Y = S[g], T[g]
        RX = jnp.zeros((8, 128), F32)
        RY = RX
        for s in range(8):
            root = lax.rsqrt(down(c[s], s))
            inv = root * root
            xr, yr = down(X, s), down(Y, s)
            me = sub == s
            RX = jnp.where(me, xr * root, RX)
            RY = jnp.where(me, yr * root, RY)
            qx, qy = xr * inv, yr * inv
            X = jnp.where(me, qx, X - c[s] * qx)
            Y = jnp.where(me, qy, Y - c[s] * qy)
            for u in range(s + 1, 8):
                qc = down(c[u], s) * inv
                c[u] = jnp.where(me, qc, c[u] - c[s] * qc)
        upper.append(RX)
        inverse.append(RY)
        if g in HOOK_GROUPS:
            hook()
        if g < 15:
            QX = [down(X, s) for s in range(8)]
            QY = [down(Y, s) for s in range(8)]
            for h in range(g + 1, 16):
                a, t = S[h], T[h]
                for s in range(8):
                    m = multipliers[h - g][s]
                    a = a - m * QX[s]
                    t = t - m * QY[s]
                S[h], T[h] = a, t
    return upper, inverse


def factor_tile(M, U, W128, hook, rest):
    for k in range(4):
        b = 128 * k
        upper, inverse = factor128([M[b + 8 * h:b + 8 * h + 8, b:b + 128] for h in range(16)], hook)
        if k == 0:
            rest()
        lane = lax.broadcasted_iota(jnp.int32, (8, 128), 1)
        sub = lax.broadcasted_iota(jnp.int32, (8, 128), 0)
        for h in range(16):
            U[b + 8 * h:b + 8 * h + 8, b:b + 128] = jnp.where(lane >= sub + 8 * h, upper[h], 0.0)
            W128[8 * h:8 * h + 8, :] = jnp.where(lane <= sub + 8 * h, inverse[h], 0.0)
        block = W128[...]
        M[b:b + 128, 512 + b:640 + b] = block
        R = dot3(block, M[b:b + 128, b + 128:b + 512], NN)
        M[b:b + 128, b + 128:b + 512] = R
        if k < 3:
            n = 384 - 128 * k
            U[b:b + 128, b + 128:512] = R[:, :n]
            wide = M[b:b + 128, b + 128:b + 640]
            for r in range(k + 1, 4):
                o = 128 * (r - k - 1)
                M[128 * r:128 * r + 128, b + 128:b + 640] -= dot3(R[:, o:o + 128], wide, TN)


def update_kernel(pattern, tiles, rows_in, cols_in, F_in, W_in, L_in, out, rows, cols, F, W, L1, work, sems, row_sem, tile_sem, out_sem):
    rank_row = lax.axis_index("row")
    rank_col = lax.axis_index("col")

    early = [
        pltpu.make_async_copy(W_in, W, sems.at[0]),
        pltpu.make_async_copy(L_in, L1, sems.at[1]),
        pltpu.make_async_copy(cols_in, cols, sems.at[2]),
    ]
    F_copy = pltpu.make_async_copy(F_in.at[jnp.minimum(rank_col, 1)], F, sems.at[3])

    def row_load(s):
        return pltpu.make_async_copy(rows_in.at[:, s], rows.at[:, s], row_sem.at[s])

    def tile_load(s):
        return pltpu.make_async_copy(tiles.at[s], work.at[s], tile_sem.at[s])

    for load in early:
        load.start()
    for s in range(SLOTS):
        row_load(s).start()
        tile_load(s).start()
        if s == 0:
            @pl.when((rank_row == rank_col) & (rank_col < 2))
            def _():
                F_copy.start()

    def used(panel, i):
        return jnp.where(i > panel, pattern[panel, i], 0)

    def solve(a, w):
        return dot1(a, W[w], NT)

    for load in early:
        load.wait()

    for k in range(2):
        j = rank_col + 16 * k

        @pl.when(used(0, j) > 0)
        def _():
            cols[0, k] = solve(cols[0, k], 0).astype(BF16)

        @pl.when(used(1, j) > 0)
        def _():
            @pl.when(used(0, j) > 0)
            def _():
                cols[1, k] = (cols[1, k].astype(F32) - dot1(cols[0, k], L1[...], NT)).astype(BF16)
            cols[1, k] = solve(cols[1, k], 1).astype(BF16)

    def one_row(s, carry):
        i = rank_row + 8 * s
        row_load(s).wait()
        tile_load(s).wait()

        @pl.when((rank_col < 2) & (i > rank_col))
        def _():
            work[s, 0] = rows[jnp.minimum(rank_col, 1), s].astype(F32)

        for k in range(2):
            j = rank_col + 16 * k
            for p in range(2):
                on = (j > 1) & (i >= j) & (used(p, i) > 0) & (used(p, j) > 0)

                @pl.when(on)
                def _():
                    work[s, k] -= dot1(rows[p, s], cols[p, k], NT)

        @pl.when((s == 0) & (rank_row == rank_col) & (rank_col < 2))
        def _():
            F_copy.wait()
            work[0, 0] = F[...].T

        pltpu.make_async_copy(work.at[s], out.at[s], out_sem.at[s]).start()
        return carry

    lax.fori_loop(0, SLOTS, one_row, 0)
    for s in range(SLOTS):
        pltpu.make_async_copy(work.at[s], out.at[s], out_sem.at[s]).wait()


def update(pattern, tiles, *found):
    hbm = pl.BlockSpec(memory_space=pl.ANY)
    return pl.pallas_call(
        update_kernel,
        out_shape=jax.ShapeDtypeStruct(tiles.shape, F32),
        in_specs=[pl.BlockSpec(memory_space=pltpu.SMEM)] + [hbm] * 6,
        out_specs=hbm,
        scratch_shapes=[
            pltpu.VMEM((2, SLOTS, B, B), BF16),
            pltpu.VMEM((2, 2, B, B), BF16),
            pltpu.VMEM((B, B), F32),
            pltpu.VMEM((2, B, B), BF16),
            pltpu.VMEM((B, B), BF16),
            pltpu.VMEM((SLOTS, 2, B, B), F32),
            pltpu.SemaphoreType.DMA((4,)),
            pltpu.SemaphoreType.DMA((SLOTS,)),
            pltpu.SemaphoreType.DMA((SLOTS,)),
            pltpu.SemaphoreType.DMA((SLOTS,)),
        ],
        compiler_params=pltpu.CompilerParams(vmem_limit_bytes=48 << 20),
        name="update",
    )(pattern, tiles, *found)


def per_device(tiles, pattern):
    rows, cols, factors, inverses, lead = front(pattern, tiles)
    return update(
        pattern, tiles, rows, cols.reshape(2, 2, B, B), factors, inverses, lead)


def solution(mesh):
    placed = P("row", "col", None, None)
    return jax.shard_map(
        per_device,
        mesh=mesh,
        in_specs=(placed, P()),
        out_specs=placed,
        check_vma=False,
    )
```
